32 devices in a mesh: dp: 4 (over z), pocket: 8 (over y, x, core).
Axes of the slice: x: 2, y: 2, z: 4, core: 2. Of those that a mesh axis runs over, the one named last changes fastest.
Arguments:
- atoms: bfloat16 [256, 128, 768], P(('dp', 'pocket')), may hold values from -6 to 6
- distance_bins: int32 [256, 128, 128], P(('dp', 'pocket')), may hold values from 0 to 31
- bonds: int32 [256, 128, 128], P(('dp', 'pocket')), may hold values 0 or 1
- molecule: int32 [256, 128], P(('dp', 'pocket')), may hold values from 0 to 3, never falling along the last dimension, each value on 1 to 64 neighbouring positions
- block_counts: int32 [4, 8], P('dp', 'pocket'), may hold values from 1 to 8, as said below
- block_scaffold: int32 [256], replicated, may hold values from 0 to 8191
- pocket_ids: int32 [8192, 4], replicated, may hold values from 0 to 7, as said below
- pocket_keys: bfloat16 [1024, 768], P('pocket'), may hold values from -6 to 6
- pocket_values: bfloat16 [1024, 768], P('pocket'), may hold values from -6 to 6
- pocket_bias: bfloat16 [12, 1024], P(None, 'pocket'), may hold values from -4 to 320
- bin_table: float32 [12, 32], replicated, may hold values from -4 to 320
- bond_weight: float32 [12], replicated, may hold values from 0.5 to 2.5
- w_query: bfloat16 [768, 768], replicated, may hold values from -0.21875 to 0.21875
- w_key: bfloat16 [768, 768], replicated, may hold values from -0.21875 to 0.21875
- w_value: bfloat16 [768, 768], replicated, may hold values from -0.21875 to 0.21875
- w_out: bfloat16 [768, 768], replicated, may hold values from -0.21875 to 0.21875
- w_cross_query: bfloat16 [768, 768], replicated, may hold values from -0.21875 to 0.21875
- w_cross_out: bfloat16 [768, 768], replicated, may hold values from -0.21875 to 0.21875
- cotangent: bfloat16 [128, 128, 768], P(('dp', 'pocket')), may hold values from -6 to 6
Outputs:
- updated: bfloat16 [128, 128, 768], P(('dp', 'pocket'))
- weight_grads: bfloat16 [6, 768, 768], replicated
The draws below stay inside these ranges and needn't reach their ends.
Inputs may be any that keep to these rules, and one draw needn't show every extreme that they name: `block_counts`: every column sums to 16, and in every column one device has exactly 8 live blocks. `pocket_ids`: each row names 4 different pocket blocks.
All inputs are finite; a program needn't handle non-finite values. No bound on the sum of `bonds` on one device may be relied on, other than what follows from the above.
Results may differ from the reference program's by a relative error of at most 0.012.
The reference program's roundings to bfloat16 on the way count: a program that leaves them out, or rounds other values in their place, can miss the bound.
Values may be sent and summed in bfloat16 or wider, within the bound.
A program may use at most 128 MiB of HBM per device.

```python
import math
import jax
import jax.numpy as jnp
import numpy as np
from jax import lax

D = 768
H = 12
A = 128
NBINS = 32
MOLS = 4
KP = 4
SCAFFOLDS = 8192
BAL = 4
CAP = 8
DP_DEVS = 4
POCKET_DEVS = 8
SLOTS = 256
BLOCKS = 128
ROWS = 16384
PBLK = 8
PATOMS = 1024


def draw_block_counts(key, part):
    heavy_key = jax.random.fold_in(key, 11)
    fill_key = jax.random.fold_in(key, 12)
    device_rows = lax.broadcasted_iota(jnp.int32, (DP_DEVS, POCKET_DEVS), 0)
    heavy = jax.random.randint(heavy_key, (1, POCKET_DEVS), 0, DP_DEVS)
    start_counts = jnp.where(device_rows == heavy, CAP, 1).astype(jnp.int32)
    extra_units = DP_DEVS * BAL - CAP - (DP_DEVS - 1)

    def add_one(step_index, current):
        draws = jax.random.randint(jax.random.fold_in(fill_key, step_index), (DP_DEVS, POCKET_DEVS), 0, 1 << 20)
        ranked = draws * DP_DEVS + device_rows
        ranked = jnp.where(current < CAP, ranked, -1)
        best_score = jnp.max(ranked, axis=0, keepdims=True)
        return current + (ranked == best_score).astype(jnp.int32)
    return lax.fori_loop(0, extra_units, add_one, start_counts)


def draw_pocket_ids(key, part):
    draws = jax.random.randint(jax.random.fold_in(key, 21), (SCAFFOLDS, PBLK), 0, 1 << 16)
    ranked = draws * PBLK + lax.broadcasted_iota(jnp.int32, (SCAFFOLDS, PBLK), 1)
    ordering = jnp.argsort(ranked, axis=1, stable=True)
    return ordering[:, :KP].astype(jnp.int32)


def draw_bin_table(key, part):
    base_key = jax.random.fold_in(key, 31)
    values = jnp.clip(jax.random.normal(base_key, (H, NBINS), jnp.float32), -4.0, 4.0)
    return values


def draw_pocket_bias(key, part):
    base_key = jax.random.fold_in(key, 51)
    values = jnp.clip(jax.random.normal(base_key, (H, PATOMS), jnp.float32), -4.0, 4.0)
    return values.astype(jnp.bfloat16)


def set_ends(values, key, least, largest):
    longest = values.shape.index(max(values.shape))
    spots = []
    for shift in (0, 1):
        where = [jax.random.randint(jax.random.fold_in(key, axis), (), 0, length) for axis, length in enumerate(values.shape)]
        where[longest] = (where[longest] + shift) % values.shape[longest]
        spots.append(tuple(where))
    return values.at[spots[0]].set(least).at[spots[1]].set(largest)


def block_scale(stream_key, shape, split, low, high):
    factor_of, own = 1.0, jax.random.fold_in(stream_key, 6)
    for dim, shards_of in split:
        steps = jnp.exp(jax.random.uniform(jax.random.fold_in(own, dim), (shards_of,), jnp.float32, low / len(split), high / len(split)))
        factor_of = factor_of * jnp.repeat(steps, shape[dim] // shards_of).reshape([-1 if axis == dim else 1 for axis in range(len(shape))])
    return factor_of


def profile(amount, total, reach, skew):
    loads = [(1 << 20) // math.isqrt(grade ** skew) + 1 for grade in range(2, amount + 1)]
    surplus, given = total - reach - (amount - 1), [1] * (amount - 1)
    while surplus > 0:
        movable = [i for i in range(amount - 1) if given[i] < reach]
        mass, left = sum([loads[i] for i in movable]), surplus
        for i in movable:
            more = min(reach - given[i], max(1, left * loads[i] // mass), surplus)
            given[i] = given[i] + more
            surplus = surplus - more
    return np.array([reach] + given)


def ragged(own_key, count, total, most, slope):
    if count == 2:
        one = jax.random.randint(own_key, (), max(1, total - most), min(most, total - 1) + 1)
        return jnp.stack([one, total - one])
    lengths = jnp.asarray(profile(count, total, most, slope), jnp.int32)
    couples = (count - 1) // 2
    source_of, receiver = lengths[1:1 + 2 * couples:2], lengths[2:2 + 2 * couples:2]
    margin = jnp.minimum(source_of - 1, most - receiver)
    shifted = jax.random.randint(jax.random.fold_in(own_key, 1), (couples,), 0, 1 << 20) % (margin + 1)
    lengths = lengths.at[1:1 + 2 * couples:2].set(source_of - shifted).at[2:2 + 2 * couples:2].set(receiver + shifted)
    return lengths[jax.random.permutation(jax.random.fold_in(own_key, 2), count)]


def scatter_about(rng, shape, scale, limit, shards=(), kind=jnp.bfloat16):
    values = jax.random.normal(rng, shape, jnp.float32) * scale
    if len(shards) > 0:
        values = block_scale(rng, shape, shards, -0.22, 0.18) * values
    return jnp.clip(values, min=-limit, max=limit).astype(kind)


def setup_inputs(seed: int = 0) -> dict:
    seeds = jax.random.split(jax.random.key(seed), 20)
    atoms = scatter_about(seeds[0], (SLOTS, A, D), 1.0, 6.0, ((0, 32),))
    distance_bins = set_ends(jax.random.randint(seeds[1], (SLOTS, A, A), 0, NBINS), jax.random.fold_in(seeds[1], 1), 0, NBINS - 1).astype(jnp.int32)
    bonds = set_ends((jax.random.randint(seeds[2], (SLOTS, A, A), 0, 8) < 1).astype(jnp.int32), jax.random.fold_in(seeds[2], 1), 0, 1)
    molecule = jax.vmap(lambda own: jnp.searchsorted(jnp.cumsum(ragged(own, MOLS, A, A // 2, 2)), jnp.arange(A), side="right"))(jax.random.split(seeds[3], SLOTS)).reshape((SLOTS, A)).astype(jnp.int32)
    block_counts = draw_block_counts(jax.random.fold_in(seeds[19], 71), 0)
    block_scaffold = set_ends(jax.random.randint(seeds[5], (SLOTS,), 0, SCAFFOLDS), jax.random.fold_in(seeds[5], 1), 0, SCAFFOLDS - 1).astype(jnp.int32)
    pocket_ids = draw_pocket_ids(jax.random.fold_in(seeds[19], 71), 0)
    pocket_keys = scatter_about(seeds[7], (PATOMS, D), 1.0, 6.0, ((0, 8),))
    pocket_values = scatter_about(seeds[8], (PATOMS, D), 1.0, 6.0, ((0, 8),))
    pocket_bias = draw_pocket_bias(jax.random.fold_in(seeds[19], 71), 0)
    bin_table = draw_bin_table(jax.random.fold_in(seeds[19], 71), 0)
    bond_weight = jnp.clip(jax.random.uniform(seeds[11], (H,), jnp.float32, 0.5, 2.5), 0.5, 2.5)
    w_query = scatter_about(seeds[12], (D, D), D ** -0.5, 0.21875)
    w_key = scatter_about(seeds[13], (D, D), D ** -0.5, 0.21875)
    w_value = scatter_about(seeds[14], (D, D), D ** -0.5, 0.21875)
    w_out = scatter_about(seeds[15], (D, D), D ** -0.5, 0.21875)
    w_cross_query = scatter_about(seeds[16], (D, D), D ** -0.5, 0.21875)
    w_cross_out = scatter_about(seeds[17], (D, D), D ** -0.5, 0.21875)
    cotangent = scatter_about(seeds[18], (BLOCKS, A, D), 1.0, 6.0, ((0, 32),))
    return {"atoms": atoms, "distance_bins": distance_bins, "bonds": bonds, "molecule": molecule, "block_counts": block_counts, "block_scaffold": block_scaffold, "pocket_ids": pocket_ids, "pocket_keys": pocket_keys, "pocket_values": pocket_values, "pocket_bias": pocket_bias, "bin_table": bin_table, "bond_weight": bond_weight, "w_query": w_query, "w_key": w_key, "w_value": w_value, "w_out": w_out, "w_cross_query": w_cross_query, "w_cross_out": w_cross_out, "cotangent": cotangent}


masked_value = -30000.0

def pair_bias(bin_rows, bond_rows, molecule_rows, bin_table, bond_weight):
    bin_count = bin_table.shape[1]
    levels = lax.broadcasted_iota(jnp.int32, (1, 1, 1, bin_count), 3)
    one_hot = (bin_rows[..., None] == levels).astype(jnp.float32)
    looked_up = jnp.einsum('cijn,hn->chij', one_hot, bin_table.astype(jnp.float32), precision=lax.Precision.HIGHEST)
    bonded = looked_up + bond_weight.astype(jnp.float32)[None, :, None, None] * bond_rows[:, None, :, :].astype(jnp.float32)
    same_molecule = molecule_rows[:, None, :, None] == molecule_rows[:, None, None, :]
    return jnp.where(same_molecule, bonded, masked_value).astype(jnp.bfloat16)

def project_rows(left, weight):
    flat = left.reshape(-1, left.shape[-1])
    result = jnp.dot(flat, weight, preferred_element_type=jnp.float32)
    return result.reshape(left.shape[:-1] + (weight.shape[1],))

def project_back(left, weight):
    flat = left.reshape(-1, left.shape[-1])
    result = lax.dot_general(flat, weight, (((1,), (1,)), ((), ())), preferred_element_type=jnp.float32)
    return result.reshape(left.shape[:-1] + (weight.shape[0],))

def weight_product(left, right):
    return lax.dot_general(left.reshape(-1, left.shape[-1]), right.reshape(-1, right.shape[-1]), (((0,), (0,)), ((), ())), preferred_element_type=jnp.float32)

def softmax_rows(scores):
    highest = lax.optimization_barrier(jnp.max(scores, axis=-1, keepdims=True))
    expsum = jnp.exp(scores - highest)
    return expsum / lax.optimization_barrier(jnp.sum(expsum, axis=-1, keepdims=True))

def split_heads(matrix, heads):
    return matrix.reshape(matrix.shape[0], matrix.shape[1], heads, matrix.shape[2] // heads)

def einsum_wide(form, left, right):
    return jnp.einsum(form, left.astype(jnp.float32), right.astype(jnp.float32))

def layer_pass(block_atoms, block_bias, cross_keys, cross_values, cross_bias, cotangent_rows, weights, heads):
    w_query, w_key, w_value, w_out, w_cquery, w_cout = weights
    block_count, row_count, width = block_atoms.shape
    scale = 1.0 / math.sqrt(width // heads)
    query_rows = project_rows(block_atoms, w_query).astype(jnp.bfloat16)
    key_rows = project_rows(block_atoms, w_key).astype(jnp.bfloat16)
    value_rows = project_rows(block_atoms, w_value).astype(jnp.bfloat16)
    query_heads = split_heads(query_rows, heads)
    key_heads = split_heads(key_rows, heads)
    value_heads = split_heads(value_rows, heads)
    scores = einsum_wide('bihd,bjhd->bhij', query_heads, key_heads) * scale + block_bias.astype(jnp.float32)
    probs = softmax_rows(scores)
    probs_rounded = probs.astype(jnp.bfloat16)
    attended = einsum_wide('bhij,bjhd->bihd', probs_rounded, value_heads).reshape(block_count, row_count, width).astype(jnp.bfloat16)
    middle = (block_atoms.astype(jnp.float32) + project_rows(attended, w_out)).astype(jnp.bfloat16)
    cross_query = project_rows(middle, w_cquery).astype(jnp.bfloat16)
    cquery_heads = split_heads(cross_query, heads)
    ckey_heads = split_heads(cross_keys, heads)
    cvalue_heads = split_heads(cross_values, heads)
    cross_scores = einsum_wide('bihd,bthd->bhit', cquery_heads, ckey_heads) * scale + cross_bias.astype(jnp.float32)[:, :, None, :]
    cross_probs = softmax_rows(cross_scores)
    cross_rounded = cross_probs.astype(jnp.bfloat16)
    cross_attended = einsum_wide('bhit,bthd->bihd', cross_rounded, cvalue_heads).reshape(block_count, row_count, width).astype(jnp.bfloat16)
    updated = (middle.astype(jnp.float32) + project_rows(cross_attended, w_cout)).astype(jnp.bfloat16)
    grad_cout = weight_product(cross_attended, cotangent_rows)
    d_cross = project_back(cotangent_rows, w_cout).astype(jnp.bfloat16)
    d_cross_probs = einsum_wide('bihd,bthd->bhit', split_heads(d_cross, heads), cvalue_heads)
    d_cross_scores = (cross_probs * (d_cross_probs - lax.optimization_barrier(jnp.sum(cross_probs * d_cross_probs, axis=-1, keepdims=True))) * scale).astype(jnp.bfloat16)
    d_cross_query = einsum_wide('bhit,bthd->bihd', d_cross_scores, ckey_heads).reshape(block_count, row_count, width).astype(jnp.bfloat16)
    grad_cquery = weight_product(middle, d_cross_query)
    d_middle = (cotangent_rows.astype(jnp.float32) + project_back(d_cross_query, w_cquery)).astype(jnp.bfloat16)
    grad_out = weight_product(attended, d_middle)
    d_attended = project_back(d_middle, w_out).astype(jnp.bfloat16)
    dattn_heads = split_heads(d_attended, heads)
    d_probs = einsum_wide('bihd,bjhd->bhij', dattn_heads, value_heads)
    d_scores = (probs * (d_probs - lax.optimization_barrier(jnp.sum(probs * d_probs, axis=-1, keepdims=True))) * scale).astype(jnp.bfloat16)
    d_query = einsum_wide('bhij,bjhd->bihd', d_scores, key_heads).reshape(block_count, row_count, width).astype(jnp.bfloat16)
    d_key = einsum_wide('bhij,bihd->bjhd', d_scores, query_heads).reshape(block_count, row_count, width).astype(jnp.bfloat16)
    d_value = einsum_wide('bhij,bihd->bjhd', probs_rounded, dattn_heads).reshape(block_count, row_count, width).astype(jnp.bfloat16)
    grad_query = weight_product(block_atoms, d_query)
    grad_key = weight_product(block_atoms, d_key)
    grad_value = weight_product(block_atoms, d_value)
    grads = jnp.stack([grad_query, grad_key, grad_value, grad_out, grad_cquery, grad_cout])
    return (updated, grads)

def reference(atoms, distance_bins, bonds, molecule, block_counts, block_scaffold, pocket_ids, pocket_keys, pocket_values, pocket_bias, bin_table, bond_weight, w_query, w_key, w_value, w_out, w_cross_query, w_cross_out, cotangent):
    counts = block_counts.astype(jnp.int32)
    ends = jnp.cumsum(counts, axis=0).astype(jnp.int32)
    starts = (ends - counts).astype(jnp.int32)
    block_index = jnp.arange(BLOCKS, dtype=jnp.int32)
    target_device = block_index // (POCKET_DEVS * BAL)
    group_index = block_index // BAL % POCKET_DEVS
    live_rank = block_index % BAL * DP_DEVS + target_device
    source_device = lax.optimization_barrier(jnp.sum((ends[:, group_index] <= live_rank[None, :]).astype(jnp.int32), axis=0)).astype(jnp.int32)
    source_slot = ((source_device * POCKET_DEVS + group_index) * CAP + live_rank - starts[source_device, group_index]).astype(jnp.int32)
    key_blocks = pocket_keys.reshape(PBLK, A, D)
    value_blocks = pocket_values.reshape(PBLK, A, D)
    bias_blocks = pocket_bias.reshape(H, PBLK, A)
    weights = (w_query, w_key, w_value, w_out, w_cross_query, w_cross_out)

    def one_device(total, inputs):
        slot_rows, cotangent_rows = inputs
        block_bias = pair_bias(distance_bins[slot_rows], bonds[slot_rows], molecule[slot_rows], bin_table, bond_weight)
        chosen = pocket_ids[block_scaffold[slot_rows]]
        cross_keys = key_blocks[chosen].reshape(BAL, KP * A, D)
        cross_values = value_blocks[chosen].reshape(BAL, KP * A, D)
        cross_bias = jnp.transpose(bias_blocks[:, chosen], (1, 0, 2, 3)).reshape(BAL, H, KP * A)
        updated, grads = layer_pass(atoms[slot_rows], block_bias, cross_keys, cross_values, cross_bias, cotangent_rows, weights, H)
        return (total + grads, updated)
    total, updated = lax.scan(one_device, jnp.zeros((6, D, D), jnp.float32), (source_slot.reshape(-1, BAL), cotangent.reshape(-1, BAL, A, D)))
    weight_grads = (total * (1.0 / math.sqrt(ROWS))).astype(jnp.bfloat16)
    return (updated.reshape(BLOCKS, A, D), weight_grads)
```

```python
import math

import jax
import jax.numpy as jnp
from jax import lax
from jax.sharding import PartitionSpec as P

masked_value = -30000.0


def pair_bias(bin_rows, bond_rows, molecule_rows, bin_table, bond_weight):
    bin_count = bin_table.shape[1]
    levels = lax.broadcasted_iota(jnp.int32, (1, 1, 1, bin_count), 3)
    one_hot = (bin_rows[..., None] == levels).astype(jnp.float32)
    looked_up = jnp.einsum("cijn,hn->chij", one_hot, bin_table, precision=lax.Precision.HIGHEST)
    bonded = looked_up + bond_weight[None, :, None, None] * bond_rows[:, None, :, :].astype(
        jnp.float32
    )
    same_molecule = molecule_rows[:, None, :, None] == molecule_rows[:, None, None, :]
    return jnp.where(same_molecule, bonded, masked_value).astype(jnp.bfloat16)


def project_rows(left, weight):
    flat = left.reshape(-1, left.shape[-1])
    result = jnp.dot(flat, weight, preferred_element_type=jnp.float32)
    return result.reshape(left.shape[:-1] + (weight.shape[1],))


def project_back(left, weight):
    flat = left.reshape(-1, left.shape[-1])
    result = lax.dot_general(
        flat, weight, (((1,), (1,)), ((), ())), preferred_element_type=jnp.float32
    )
    return result.reshape(left.shape[:-1] + (weight.shape[0],))


def weight_product(left, right):
    return lax.dot_general(
        left.reshape(-1, left.shape[-1]),
        right.reshape(-1, right.shape[-1]),
        (((0,), (0,)), ((), ())),
        preferred_element_type=jnp.float32,
    )


def softmax_rows(scores):
    highest = jnp.max(scores, axis=-1, keepdims=True)
    expsum = jnp.exp(scores - highest)
    return expsum / jnp.sum(expsum, axis=-1, keepdims=True)


def split_heads(matrix, heads):
    return matrix.reshape(matrix.shape[0], matrix.shape[1], heads, matrix.shape[2] // heads)


def einsum_mixed(form, left, right):
    return jnp.einsum(form, left, right, preferred_element_type=jnp.float32)


def layer_pass(
    block_atoms, block_bias, cross_keys, cross_values, cross_bias, cotangent_rows, weights, heads
):
    w_query, w_key, w_value, w_out, w_cquery, w_cout = weights
    block_count, row_count, width = block_atoms.shape
    scale = 1.0 / math.sqrt(width // heads)
    query_rows = project_rows(block_atoms, w_query).astype(jnp.bfloat16)
    key_rows = project_rows(block_atoms, w_key).astype(jnp.bfloat16)
    value_rows = project_rows(block_atoms, w_value).astype(jnp.bfloat16)
    query_heads = split_heads(query_rows, heads)
    key_heads = split_heads(key_rows, heads)
    value_heads = split_heads(value_rows, heads)
    scores = einsum_mixed("bihd,bjhd->bhij", query_heads, key_heads) * scale + block_bias.astype(
        jnp.float32
    )
    probs = softmax_rows(scores)
    probs_rounded = probs.astype(jnp.bfloat16)
    attended = (
        einsum_mixed("bhij,bjhd->bihd", probs_rounded, value_heads)
        .reshape(block_count, row_count, width)
        .astype(jnp.bfloat16)
    )
    middle = (block_atoms.astype(jnp.float32) + project_rows(attended, w_out)).astype(jnp.bfloat16)
    cross_query = project_rows(middle, w_cquery).astype(jnp.bfloat16)
    cquery_heads = split_heads(cross_query, heads)
    ckey_heads = split_heads(cross_keys, heads)
    cvalue_heads = split_heads(cross_values, heads)
    cross_scores = (
        einsum_mixed("bihd,bthd->bhit", cquery_heads, ckey_heads) * scale
        + cross_bias.astype(jnp.float32)[:, :, None, :]
    )
    cross_probs = softmax_rows(cross_scores)
    cross_rounded = cross_probs.astype(jnp.bfloat16)
    cross_attended = (
        einsum_mixed("bhit,bthd->bihd", cross_rounded, cvalue_heads)
        .reshape(block_count, row_count, width)
        .astype(jnp.bfloat16)
    )
    updated = (middle.astype(jnp.float32) + project_rows(cross_attended, w_cout)).astype(
        jnp.bfloat16
    )
    grad_cout = weight_product(cross_attended, cotangent_rows)
    d_cross = project_back(cotangent_rows, w_cout).astype(jnp.bfloat16)
    d_cross_probs = einsum_mixed("bihd,bthd->bhit", split_heads(d_cross, heads), cvalue_heads)
    d_cross_scores = (
        cross_probs
        * (d_cross_probs - jnp.sum(cross_probs * d_cross_probs, axis=-1, keepdims=True))
        * scale
    ).astype(jnp.bfloat16)
    d_cross_query = (
        einsum_mixed("bhit,bthd->bihd", d_cross_scores, ckey_heads)
        .reshape(block_count, row_count, width)
        .astype(jnp.bfloat16)
    )
    grad_cquery = weight_product(middle, d_cross_query)
    d_middle = (cotangent_rows.astype(jnp.float32) + project_back(d_cross_query, w_cquery)).astype(
        jnp.bfloat16
    )
    grad_out = weight_product(attended, d_middle)
    d_attended = project_back(d_middle, w_out).astype(jnp.bfloat16)
    dattn_heads = split_heads(d_attended, heads)
    d_probs = einsum_mixed("bihd,bjhd->bhij", dattn_heads, value_heads)
    d_scores = (
        probs * (d_probs - jnp.sum(probs * d_probs, axis=-1, keepdims=True)) * scale
    ).astype(jnp.bfloat16)
    d_query = (
        einsum_mixed("bhij,bjhd->bihd", d_scores, key_heads)
        .reshape(block_count, row_count, width)
        .astype(jnp.bfloat16)
    )
    d_key = (
        einsum_mixed("bhij,bihd->bjhd", d_scores, query_heads)
        .reshape(block_count, row_count, width)
        .astype(jnp.bfloat16)
    )
    d_value = (
        einsum_mixed("bhij,bihd->bjhd", probs_rounded, dattn_heads)
        .reshape(block_count, row_count, width)
        .astype(jnp.bfloat16)
    )
    grad_query = weight_product(block_atoms, d_query)
    grad_key = weight_product(block_atoms, d_key)
    grad_value = weight_product(block_atoms, d_value)
    grads = jnp.stack([grad_query, grad_key, grad_value, grad_out, grad_cquery, grad_cout])
    return (updated, grads)


def pick(array, index):
    rows = [lax.dynamic_slice_in_dim(array, index[i], 1, 0) for i in range(index.shape[0])]
    return jnp.concatenate(rows, axis=0)


def on_device(
    atoms,
    distance_bins,
    bonds,
    molecule,
    block_counts,
    block_scaffold,
    pocket_ids,
    pocket_keys,
    pocket_values,
    pocket_bias,
    bin_table,
    bond_weight,
    w_query,
    w_key,
    w_value,
    w_out,
    w_cross_query,
    w_cross_out,
    cotangent,
):
    dp_count = lax.axis_size("dp")
    pocket_count = lax.axis_size("pocket")
    capacity = atoms.shape[0]
    balanced = cotangent.shape[0]
    row_count = atoms.shape[1]
    width = atoms.shape[2]
    heads = bin_table.shape[0]
    per_target = capacity // dp_count
    counts = lax.all_gather(block_counts.reshape(1), "dp", axis=0, tiled=True)
    places = lax.broadcasted_iota(jnp.int32, (dp_count, dp_count), 0)
    before = places > lax.broadcasted_iota(jnp.int32, (dp_count, dp_count), 1)
    offsets = jnp.sum(jnp.where(before, counts[None, :], 0), axis=1)
    own_device = lax.axis_index("dp")
    own_column = lax.axis_index("pocket")
    own_offset = offsets[own_device]
    own_count = counts[own_device]
    target_rows = lax.broadcasted_iota(jnp.int32, (dp_count, per_target), 0)
    turn_index = lax.broadcasted_iota(jnp.int32, (dp_count, per_target), 1)
    outgoing = jnp.mod(target_rows - own_offset, dp_count) + dp_count * turn_index
    picked = jnp.where(outgoing < own_count, outgoing, 0).reshape(-1)
    source_offset = offsets[:, None]
    source_count = counts[:, None]
    incoming = jnp.mod(own_device - source_offset, dp_count) + dp_count * turn_index
    usable = incoming < source_count
    landing = (source_offset + incoming) // dp_count
    wanted = lax.broadcasted_iota(jnp.int32, (balanced, 1), 0)
    matches = (landing.reshape(1, -1) == wanted) & usable.reshape(1, -1)
    received_index = lax.broadcasted_iota(jnp.int32, (balanced, dp_count * per_target), 1)
    position = jnp.sum(jnp.where(matches, received_index, 0), axis=1)
    local_bias = pair_bias(distance_bins, bonds, molecule, bin_table, bond_weight)
    got_atoms, got_bias = (
        lax.all_to_all(pick(atoms, picked), "dp", split_axis=0, concat_axis=0, tiled=True),
        lax.all_to_all(pick(local_bias, picked), "dp", split_axis=0, concat_axis=0, tiled=True),
    )
    block_atoms = pick(got_atoms, position)
    block_bias = pick(got_bias, position)
    anchor = ((target_rows * pocket_count + own_column) * capacity + incoming).reshape(-1)
    anchor = pick(anchor, position)
    scaffold = pick(block_scaffold, anchor)
    all_keys, all_values, all_bias = (
        lax.all_gather(pocket_keys, "pocket", axis=0, tiled=True),
        lax.all_gather(pocket_values, "pocket", axis=0, tiled=True),
        lax.all_gather(pocket_bias, "pocket", axis=1, tiled=True),
    )
    pocket_blocks = all_keys.shape[0] // row_count
    chosen = pick(pocket_ids, scaffold)
    flat_chosen = chosen.reshape(-1)
    cross_keys = pick(all_keys.reshape(pocket_blocks, row_count, width), flat_chosen).reshape(
        balanced, -1, width
    )
    cross_values = pick(all_values.reshape(pocket_blocks, row_count, width), flat_chosen).reshape(
        balanced, -1, width
    )
    cross_bias = jnp.transpose(
        pick(
            jnp.transpose(all_bias.reshape(heads, pocket_blocks, row_count), (1, 0, 2)), flat_chosen
        ).reshape(chosen.shape + (heads, row_count)),
        (0, 2, 1, 3),
    ).reshape(balanced, heads, -1)
    per_pass = math.gcd(balanced, max(1, 512 // row_count))
    passes = balanced // per_pass
    weights = (w_query, w_key, w_value, w_out, w_cross_query, w_cross_out)

    def regroup(matrix):
        return matrix.reshape((passes, per_pass) + matrix.shape[1:])

    def one_pass(total, inputs):
        pass_atoms, pass_bias, pass_keys, pass_values, pass_cross_bias, pass_cotangent = inputs
        updated_rows, grads = layer_pass(
            pass_atoms,
            pass_bias,
            pass_keys,
            pass_values,
            pass_cross_bias,
            pass_cotangent,
            weights,
            heads,
        )
        return (total + grads, updated_rows)

    start_total = jnp.zeros((6, width, width), jnp.float32)
    total, updated = lax.scan(
        one_pass,
        start_total,
        (
            regroup(block_atoms),
            regroup(block_bias),
            regroup(cross_keys),
            regroup(cross_values),
            regroup(cross_bias),
            regroup(cotangent),
        ),
    )
    updated = updated.reshape(cotangent.shape)
    scale = 1.0 / math.sqrt(balanced * row_count * dp_count * pocket_count)
    weight_grads = (lax.psum(total, ("dp", "pocket")) * scale).astype(jnp.bfloat16)
    return (updated, weight_grads)


def solution(mesh):
    return jax.shard_map(
        on_device,
        mesh=mesh,
        in_specs=(
            P(("dp", "pocket"), None, None),
            P(("dp", "pocket"), None, None),
            P(("dp", "pocket"), None, None),
            P(("dp", "pocket"), None),
            P("dp", "pocket"),
            P(),
            P(),
            P("pocket", None),
            P("pocket", None),
            P(None, "pocket"),
            P(),
            P(),
            P(),
            P(),
            P(),
            P(),
            P(),
            P(),
            P(("dp", "pocket"), None, None),
        ),
        out_specs=(P(("dp", "pocket"), None, None), P()),
        check_vma=False,
    )
```

```python
import math

import jax
import jax.numpy as jnp
from jax import lax
from jax.experimental import pallas as pl
from jax.experimental.pallas import tpu as pltpu
from jax.sharding import PartitionSpec as P

masked_value = -30000.0
half = 64
lanes = 128
extra_rows = 16
vmem_bytes = 60 * 1024 * 1024


def pick(array, index):
    rows = [lax.dynamic_slice_in_dim(array, index[i], 1, 0) for i in range(index.shape[0])]
    return jnp.concatenate(rows, axis=0)


def dot(left, right):
    return lax.dot_general(left, right, (((1,), (0,)), ((), ())), preferred_element_type=jnp.float32)


def dot_rows(left, right):
    return lax.dot_general(left, right, (((1,), (1,)), ((), ())), preferred_element_type=jnp.float32)


def dot_columns(left, right):
    return lax.dot_general(left, right, (((0,), (0,)), ((), ())), preferred_element_type=jnp.float32)


def narrow(values):
    return values.astype(jnp.bfloat16)


def pack_kernel(picked, atoms, bins, bonds, molecule, payload):
    rows, width = atoms.shape[1], atoms.shape[2]
    payload[0, :rows, :width] = atoms[0]
    payload[0, :rows, width : width + lanes] = narrow(bins[0].astype(jnp.float32))
    payload[0, :rows, width + lanes :] = narrow(bonds[0].astype(jnp.float32))
    payload[0, rows:, :] = jnp.zeros((extra_rows, width + 2 * lanes), jnp.bfloat16)
    molecule_rows = jnp.broadcast_to(molecule[0].astype(jnp.float32), (extra_rows, lanes))
    payload[0, rows:, :lanes] = narrow(molecule_rows)


def pack_blocks(picked, atoms, bins, bonds, molecule):
    _, rows, width = atoms.shape
    sent = picked.shape[0]

    def own(i, picked):
        return (picked[i], 0, 0)

    return pl.pallas_call(
        pack_kernel,
        grid_spec=pltpu.PrefetchScalarGridSpec(
            num_scalar_prefetch=1,
            grid=(sent,),
            in_specs=[
                pl.BlockSpec((1, rows, width), own),
                pl.BlockSpec((1, rows, rows), own),
                pl.BlockSpec((1, rows, rows), own),
                pl.BlockSpec((1, 1, rows), own),
            ],
            out_specs=pl.BlockSpec(
                (1, rows + extra_rows, width + 2 * lanes), lambda i, picked: (i, 0, 0)
            ),
        ),
        out_shape=jax.ShapeDtypeStruct((sent, rows + extra_rows, width + 2 * lanes), jnp.bfloat16),
        name="pack_blocks",
    )(picked, atoms, bins, bonds, molecule[:, None, :])


def both_halves(pair):
    lane = lax.broadcasted_iota(jnp.int32, (1, lanes), 1)
    first = narrow((lane < half).astype(jnp.float32))
    second = narrow((lane >= half).astype(jnp.float32))
    return jnp.concatenate([pair * first, pair * second], axis=0)


def side_by_side(stacked):
    rows = stacked.shape[0] // 2
    return jnp.concatenate([stacked[:rows], stacked[rows:]], axis=1)


def softmax_rows(scores):
    raised = jnp.exp(scores - jnp.max(scores, axis=-1, keepdims=True))
    return raised * (1.0 / jnp.sum(raised, axis=-1, keepdims=True))


def softmax_back(probs, d_probs, scale):
    inner = jnp.sum(probs * d_probs, axis=-1, keepdims=True)
    return narrow(probs * (d_probs - inner) * scale)


def layer_kernel(
    position, chosen, got, pocket, cross_bias, table, w_query, w_key, w_value, w_out, w_cquery,
    w_cout, cotangent, updated, grads, x, query, key, value, attended, middle, cquery, cattended,
    d_cross, d_cquery, d_middle, d_attended, d_query, d_key, d_value, code, probs
):
    rows = got.shape[1] - extra_rows
    width = x.shape[1]
    blocks = x.shape[0] // rows
    pairs = width // lanes
    per_block = chosen.shape[0] // blocks
    scale = 1.0 / math.sqrt(half)
    for b in range(blocks):
        block = got.at[position[b]]
        x[b * rows : (b + 1) * rows, :] = block[:rows, :width]
        bins = block[:rows, width : width + lanes].astype(jnp.float32)
        bonds = block[:rows, width + lanes :].astype(jnp.float32)
        molecule = block[rows:, :lanes].astype(jnp.float32)
        along = jnp.broadcast_to(molecule[0:1], (rows, lanes))
        live = bins + 32.0 * bonds
        code[b] = jnp.where(along == along.T, live, 64.0).astype(jnp.int32)
    query[...] = narrow(dot(x[...], w_query[...]))
    key[...] = narrow(dot(x[...], w_key[...]))
    value[...] = narrow(dot(x[...], w_value[...]))

    def place(step):
        b, p = step // pairs, step % pairs
        return b, p, pl.ds(pl.multiple_of(b * rows, rows), rows), pl.ds(pl.multiple_of(p * lanes, lanes), lanes)

    @pl.loop(0, blocks * pairs)
    def _(step):
        b, p, at, columns = place(step)
        index = code[b]
        bias = jnp.concatenate(
            [
                jnp.take_along_axis(
                    jnp.broadcast_to(table[2 * p + h], (rows, lanes)), index, axis=1, mode="promise_in_bounds"
                )
                for h in range(2)
            ],
            axis=0,
        )
        scores = dot_rows(both_halves(query[at, columns]), key[at, columns]) * scale + bias
        weights = softmax_rows(scores)
        probs[step] = weights
        rounded = side_by_side(narrow(weights))
        attended[at, columns] = narrow(dot(rounded, both_halves(value[at, columns])))

    middle[...] = narrow(x[...].astype(jnp.float32) + dot(attended[...], w_out[...]))
    cquery[...] = narrow(dot(middle[...], w_cquery[...]))
    d_cross[...] = narrow(dot_rows(cotangent[...], w_cout[...]))

    @pl.loop(0, blocks * pairs)
    def _(step):
        b, p, at, columns = place(step)
        far = pl.ds(pl.multiple_of(width + p * lanes, lanes), lanes)
        picks = [chosen[b * per_block + t] for t in range(per_block)]
        keys = jnp.concatenate([pocket[c, :rows, columns] for c in picks], axis=0)
        values = jnp.concatenate([pocket[c, :rows, far] for c in picks], axis=0)
        bias = jnp.concatenate(
            [
                jnp.broadcast_to(
                    jnp.concatenate([cross_bias[c, 2 * p + h] for c in picks], axis=1),
                    (rows, per_block * rows),
                )
                for h in range(2)
            ],
            axis=0,
        )
        weights = softmax_rows(dot_rows(both_halves(cquery[at, columns]), keys) * scale + bias)
        rounded = side_by_side(narrow(weights))
        cattended[at, columns] = narrow(dot(rounded, both_halves(values)))
        d_weights = dot_rows(both_halves(d_cross[at, columns]), values)
        d_scores = side_by_side(softmax_back(weights, d_weights, scale))
        d_cquery[at, columns] = narrow(dot(d_scores, both_halves(keys)))

    updated[...] = narrow(middle[...].astype(jnp.float32) + dot(cattended[...], w_cout[...]))
    d_middle[...] = narrow(cotangent[...].astype(jnp.float32) + dot_rows(d_cquery[...], w_cquery[...]))
    d_attended[...] = narrow(dot_rows(d_middle[...], w_out[...]))
    grads[5] = dot_columns(cattended[...], cotangent[...]).astype(grads.dtype)
    grads[4] = dot_columns(middle[...], d_cquery[...]).astype(grads.dtype)
    grads[3] = dot_columns(attended[...], d_middle[...]).astype(grads.dtype)

    @pl.loop(0, blocks * pairs)
    def _(step):
        b, p, at, columns = place(step)
        weights = probs[step]
        d_att = both_halves(d_attended[at, columns])
        d_weights = dot_rows(d_att, value[at, columns])
        d_scores = softmax_back(weights, d_weights, scale)
        d_query[at, columns] = narrow(dot(side_by_side(d_scores), both_halves(key[at, columns])))
        d_key[at, columns] = narrow(dot_columns(d_scores, both_halves(query[at, columns])))
        d_value[at, columns] = narrow(dot_columns(narrow(weights), d_att))

    grads[0] = dot_columns(x[...], d_query[...]).astype(grads.dtype)
    grads[1] = dot_columns(x[...], d_key[...]).astype(grads.dtype)
    grads[2] = dot_columns(x[...], d_value[...]).astype(grads.dtype)


def layer(position, chosen, got, pocket, cross_bias, table, weights, cotangent):
    total_rows, width = cotangent.shape
    rows = got.shape[1] - extra_rows
    blocks = total_rows // rows
    pairs = width // lanes
    whole = pl.BlockSpec(memory_space=pltpu.VMEM)
    scalar = pl.BlockSpec(memory_space=pltpu.SMEM)
    return pl.pallas_call(
        layer_kernel,
        in_specs=[scalar, scalar] + [whole] * 11,
        out_specs=[whole, whole],
        out_shape=[
            jax.ShapeDtypeStruct((total_rows, width), jnp.bfloat16),
            jax.ShapeDtypeStruct((6, width, width), jnp.bfloat16),
        ],
        scratch_shapes=[pltpu.VMEM((total_rows, width), jnp.bfloat16)] * 15
        + [
            pltpu.VMEM((blocks, rows, lanes), jnp.int32),
            pltpu.VMEM((blocks * pairs, 2 * rows, rows), jnp.float32),
        ],
        compiler_params=pltpu.CompilerParams(vmem_limit_bytes=vmem_bytes),
        name="layer",
    )(position, chosen, got, pocket, cross_bias, table, *weights, cotangent)


def on_device(
    atoms,
    distance_bins,
    bonds,
    molecule,
    block_counts,
    block_scaffold,
    pocket_ids,
    pocket_keys,
    pocket_values,
    pocket_bias,
    bin_table,
    bond_weight,
    w_query,
    w_key,
    w_value,
    w_out,
    w_cross_query,
    w_cross_out,
    cotangent,
):
    dp_count = lax.axis_size("dp")
    pocket_count = lax.axis_size("pocket")
    capacity = atoms.shape[0]
    balanced = cotangent.shape[0]
    row_count = atoms.shape[1]
    width = atoms.shape[2]
    heads = bin_table.shape[0]
    bin_count = bin_table.shape[1]
    per_target = -(-capacity // dp_count)
    pocket_rows = jnp.concatenate(
        [
            jnp.concatenate([pocket_keys, pocket_values], axis=1),
            jnp.pad(pocket_bias, ((0, extra_rows - heads), (0, 2 * width - pocket_bias.shape[1]))),
        ],
        axis=0,
    )
    pocket = lax.all_gather(pocket_rows, "pocket", axis=0)
    cross_bias = pocket[:, row_count : row_count + heads, None, :row_count].astype(jnp.float32)
    counts = lax.all_gather(block_counts.reshape(1), "dp", axis=0, tiled=True)
    places = lax.broadcasted_iota(jnp.int32, (dp_count, dp_count), 0)
    before = places > lax.broadcasted_iota(jnp.int32, (dp_count, dp_count), 1)
    offsets = jnp.sum(jnp.where(before, counts[None, :], 0), axis=1)
    own_device = lax.axis_index("dp")
    own_column = lax.axis_index("pocket")
    own_offset = offsets[own_device]
    own_count = counts[own_device]
    target_rows = lax.broadcasted_iota(jnp.int32, (dp_count, per_target), 0)
    turn_index = lax.broadcasted_iota(jnp.int32, (dp_count, per_target), 1)
    outgoing = jnp.mod(target_rows - own_offset, dp_count) + dp_count * turn_index
    picked = jnp.where(outgoing < own_count, outgoing, 0).reshape(-1)
    source_offset = offsets[:, None]
    source_count = counts[:, None]
    incoming = jnp.mod(own_device - source_offset, dp_count) + dp_count * turn_index
    usable = incoming < source_count
    landing = (source_offset + incoming) // dp_count
    wanted = lax.broadcasted_iota(jnp.int32, (balanced, 1), 0)
    matches = (landing.reshape(1, -1) == wanted) & usable.reshape(1, -1)
    received_index = lax.broadcasted_iota(jnp.int32, (balanced, dp_count * per_target), 1)
    position = jnp.sum(jnp.where(matches, received_index, 0), axis=1)
    anchors = ((target_rows * pocket_count + own_column) * capacity + incoming).reshape(1, -1)
    anchor = jnp.sum(jnp.where(matches, anchors, 0), axis=1)
    payload = pack_blocks(picked, atoms, distance_bins, bonds, molecule)
    got = lax.all_to_all(payload, "dp", split_axis=0, concat_axis=0, tiled=True)
    scaffold = pick(block_scaffold, anchor)
    ids = pocket_ids.T
    chosen = jnp.concatenate(
        [lax.dynamic_slice_in_dim(ids, scaffold[b], 1, 1)[:, 0] for b in range(balanced)]
    )
    table = jnp.concatenate(
        [
            bin_table,
            bin_table + bond_weight[:, None],
            jnp.full((heads, lanes - 2 * bin_count), masked_value, jnp.float32),
        ],
        axis=1,
    )
    table = lax.reduce_precision(table, 8, 7)[:, None, :]
    weights = (w_query, w_key, w_value, w_out, w_cross_query, w_cross_out)
    updated, grads = layer(
        position, chosen, got, pocket, cross_bias, table, weights, cotangent.reshape(-1, width)
    )
    scale = 1.0 / math.sqrt(balanced * row_count * dp_count * pocket_count)
    rows = grads.reshape(6 * width, width)
    share = lax.psum_scatter(rows, ("dp", "pocket"), scatter_dimension=0, tiled=True)
    share = (share.astype(jnp.float32) * scale).astype(jnp.bfloat16)
    weight_grads = lax.all_gather(share, ("dp", "pocket"), axis=0, tiled=True)
    return (updated.reshape(cotangent.shape), weight_grads.reshape(6, width, width))


def solution(mesh):
    return jax.shard_map(
        on_device,
        mesh=mesh,
        in_specs=(
            P(("dp", "pocket"), None, None),
            P(("dp", "pocket"), None, None),
            P(("dp", "pocket"), None, None),
            P(("dp", "pocket"), None),
            P("dp", "pocket"),
            P(),
            P(),
            P("pocket", None),
            P("pocket", None),
            P(None, "pocket"),
            P(),
            P(),
            P(),
            P(),
            P(),
            P(),
            P(),
            P(),
            P(("dp", "pocket"), None, None),
        ),
        out_specs=(P(("dp", "pocket"), None, None), P()),
        check_vma=False,
    )
```

```python
import math

import jax
import jax.numpy as jnp
from jax import lax
from jax.experimental import pallas as pl
from jax.experimental.pallas import tpu as pltpu
from jax.sharding import PartitionSpec as P

masked_value = -30000.0
half = 64
lanes = 128
extra_rows = 16
vmem_bytes = 60 * 1024 * 1024


def pick(array, index):
    rows = [lax.dynamic_slice_in_dim(array, index[i], 1, 0) for i in range(index.shape[0])]
    return jnp.concatenate(rows, axis=0)


def dot(left, right):
    return lax.dot_general(left, right, (((1,), (0,)), ((), ())), preferred_element_type=jnp.float32)


def dot_rows(left, right):
    return lax.dot_general(left, right, (((1,), (1,)), ((), ())), preferred_element_type=jnp.float32)


def dot_columns(left, right):
    return lax.dot_general(left, right, (((0,), (0,)), ((), ())), preferred_element_type=jnp.float32)


def narrow(values):
    return values.astype(jnp.bfloat16)


def pack_kernel(picked, atoms, bins, bonds, molecule, payload):
    rows, width = atoms.shape[1], atoms.shape[2]
    payload[0, :rows, :width] = atoms[0]
    payload[0, :rows, width : width + lanes] = narrow(bins[0].astype(jnp.float32))
    payload[0, :rows, width + lanes :] = narrow(bonds[0].astype(jnp.float32))
    payload[0, rows:, :] = jnp.zeros((extra_rows, width + 2 * lanes), jnp.bfloat16)
    molecule_rows = jnp.broadcast_to(molecule[0].astype(jnp.float32), (extra_rows, lanes))
    payload[0, rows:, :lanes] = narrow(molecule_rows)


def pack_blocks(picked, atoms, bins, bonds, molecule):
    _, rows, width = atoms.shape
    sent = picked.shape[0]

    def own(i, picked):
        return (picked[i], 0, 0)

    return pl.pallas_call(
        pack_kernel,
        grid_spec=pltpu.PrefetchScalarGridSpec(
            num_scalar_prefetch=1,
            grid=(sent,),
            in_specs=[
                pl.BlockSpec((1, rows, width), own),
                pl.BlockSpec((1, rows, rows), own),
                pl.BlockSpec((1, rows, rows), own),
                pl.BlockSpec((1, 1, rows), own),
            ],
            out_specs=pl.BlockSpec(
                (1, rows + extra_rows, width + 2 * lanes), lambda i, picked: (i, 0, 0)
            ),
        ),
        out_shape=jax.ShapeDtypeStruct((sent, rows + extra_rows, width + 2 * lanes), jnp.bfloat16),
        name="pack_blocks",
    )(picked, atoms, bins, bonds, molecule[:, None, :])


def both_halves(pair):
    lane = lax.broadcasted_iota(jnp.int32, (1, lanes), 1)
    first = narrow((lane < half).astype(jnp.float32))
    second = narrow((lane >= half).astype(jnp.float32))
    return jnp.concatenate([pair * first, pair * second], axis=0)


def side_by_side(stacked):
    rows = stacked.shape[0] // 2
    return jnp.concatenate([stacked[:rows], stacked[rows:]], axis=1)


def softmax_rows(scores):
    raised = jnp.exp(scores - jnp.max(scores, axis=-1, keepdims=True))
    return raised * (1.0 / jnp.sum(raised, axis=-1, keepdims=True))


def softmax_back(probs, d_probs, scale):
    inner = jnp.sum(probs * d_probs, axis=-1, keepdims=True)
    return narrow(probs * (d_probs - inner) * scale)


def layer_kernel(
    position, chosen, got, pocket, cross_bias, table, w_query, w_key, w_value, w_out, w_cquery,
    w_cout, cotangent, updated, grads, x, query, key, value, d_attended, probs, attended, middle,
    cquery, cattended, d_cross, d_cquery, d_middle, code
):
    rows = got.shape[1] - extra_rows
    width = x.shape[1]
    blocks = x.shape[0] // rows
    pairs = width // lanes
    per_block = chosen.shape[0] // blocks
    scale = 1.0 / math.sqrt(half)
    for b in range(blocks):
        block = got.at[position[b]]
        x[b * rows : (b + 1) * rows, :] = block[:rows, :width]
        bins = block[:rows, width : width + lanes].astype(jnp.float32)
        bonds = block[:rows, width + lanes :].astype(jnp.float32)
        molecule = block[rows:, :lanes].astype(jnp.float32)
        along = jnp.broadcast_to(molecule[0:1], (rows, lanes))
        live = bins + 32.0 * bonds
        code[b] = jnp.where(along == along.T, live, 64.0).astype(jnp.int32)
    query[...] = narrow(dot(x[...], w_query[...]))
    key[...] = narrow(dot(x[...], w_key[...]))
    value[...] = narrow(dot(x[...], w_value[...]))

    def place(step):
        b, p = step // pairs, step % pairs
        return b, p, pl.ds(pl.multiple_of(b * rows, rows), rows), pl.ds(pl.multiple_of(p * lanes, lanes), lanes)

    @pl.loop(0, blocks * pairs)
    def _(step):
        b, p, at, columns = place(step)
        index = code[b]
        bias = jnp.concatenate(
            [
                jnp.take_along_axis(
                    jnp.broadcast_to(table[2 * p + h], (rows, lanes)), index, axis=1, mode="promise_in_bounds"
                )
                for h in range(2)
            ],
            axis=0,
        )
        scores = dot_rows(both_halves(query[at, columns]), key[at, columns]) * scale + bias
        weights = softmax_rows(scores)
        probs[step] = weights
        rounded = side_by_side(narrow(weights))
        attended[at, columns] = narrow(dot(rounded, both_halves(value[at, columns])))

    middle[...] = narrow(x[...].astype(jnp.float32) + dot(attended[...], w_out[...]))
    cquery[...] = narrow(dot(middle[...], w_cquery[...]))
    d_cross[...] = narrow(dot_rows(cotangent[...], w_cout[...]))

    @pl.loop(0, blocks * pairs)
    def _(step):
        b, p, at, columns = place(step)
        far = pl.ds(pl.multiple_of(width + p * lanes, lanes), lanes)
        picks = [chosen[b * per_block + t] for t in range(per_block)]
        keys = jnp.concatenate([pocket[c, :rows, columns] for c in picks], axis=0)
        values = jnp.concatenate([pocket[c, :rows, far] for c in picks], axis=0)
        bias = jnp.concatenate(
            [
                jnp.broadcast_to(
                    jnp.concatenate([cross_bias[c, 2 * p + h] for c in picks], axis=1),
                    (rows, per_block * rows),
                )
                for h in range(2)
            ],
            axis=0,
        )
        weights = softmax_rows(dot_rows(both_halves(cquery[at, columns]), keys) * scale + bias)
        rounded = side_by_side(narrow(weights))
        cattended[at, columns] = narrow(dot(rounded, both_halves(values)))
        d_weights = dot_rows(both_halves(d_cross[at, columns]), values)
        d_scores = side_by_side(softmax_back(weights, d_weights, scale))
        d_cquery[at, columns] = narrow(dot(d_scores, both_halves(keys)))

    updated[...] = narrow(middle[...].astype(jnp.float32) + dot(cattended[...], w_cout[...]))
    d_middle[...] = narrow(cotangent[...].astype(jnp.float32) + dot_rows(d_cquery[...], w_cquery[...]))
    d_attended[...] = narrow(dot_rows(d_middle[...], w_out[...]))
    grads[2] = dot_columns(cattended[...], cotangent[...]).astype(grads.dtype)
    grads[1] = dot_columns(middle[...], d_cquery[...]).astype(grads.dtype)
    grads[0] = dot_columns(attended[...], d_middle[...]).astype(grads.dtype)


def self_back_kernel(x, query, key, value, d_attended, probs, grads, d_query, d_key, d_value):
    steps, rows = probs.shape[0], probs.shape[2]
    pairs = x.shape[1] // lanes
    scale = 1.0 / math.sqrt(half)

    @pl.loop(0, steps)
    def _(step):
        b, p = step // pairs, step % pairs
        at = pl.ds(pl.multiple_of(b * rows, rows), rows)
        columns = pl.ds(pl.multiple_of(p * lanes, lanes), lanes)
        weights = probs[step]
        d_att = both_halves(d_attended[at, columns])
        d_weights = dot_rows(d_att, value[at, columns])
        d_scores = softmax_back(weights, d_weights, scale)
        d_query[at, columns] = narrow(dot(side_by_side(d_scores), both_halves(key[at, columns])))
        d_key[at, columns] = narrow(dot_columns(d_scores, both_halves(query[at, columns])))
        d_value[at, columns] = narrow(dot_columns(narrow(weights), d_att))

    grads[0] = dot_columns(x[...], d_query[...]).astype(grads.dtype)
    grads[1] = dot_columns(x[...], d_key[...]).astype(grads.dtype)
    grads[2] = dot_columns(x[...], d_value[...]).astype(grads.dtype)


def layer(position, chosen, got, pocket, cross_bias, table, weights, cotangent):
    total_rows, width = cotangent.shape
    rows = got.shape[1] - extra_rows
    blocks = total_rows // rows
    pairs = width // lanes
    whole = pl.BlockSpec(memory_space=pltpu.VMEM)
    scalar = pl.BlockSpec(memory_space=pltpu.SMEM)
    flat = jax.ShapeDtypeStruct((total_rows, width), jnp.bfloat16)
    half_grads = jax.ShapeDtypeStruct((3, width, width), jnp.bfloat16)
    params = pltpu.CompilerParams(vmem_limit_bytes=vmem_bytes)
    flat_scratch = pltpu.VMEM((total_rows, width), jnp.bfloat16)
    updated, late_grads, *kept = pl.pallas_call(
        layer_kernel,
        in_specs=[scalar, scalar] + [whole] * 11,
        out_specs=[whole] * 8,
        out_shape=[flat, half_grads]
        + [flat] * 5
        + [jax.ShapeDtypeStruct((blocks * pairs, 2 * rows, rows), jnp.float32)],
        scratch_shapes=[flat_scratch] * 7 + [pltpu.VMEM((blocks, rows, lanes), jnp.int32)],
        compiler_params=params,
        name="layer",
    )(position, chosen, got, pocket, cross_bias, table, *weights, cotangent)
    early_grads = pl.pallas_call(
        self_back_kernel,
        in_specs=[whole] * 6,
        out_specs=whole,
        out_shape=half_grads,
        scratch_shapes=[flat_scratch] * 3,
        compiler_params=params,
        cost_estimate=pl.CostEstimate(
            flops=12 * total_rows * width * width, bytes_accessed=12 * total_rows * width * 2, transcendentals=0
        ),
        name="self_back",
    )(*kept)
    return updated, early_grads, late_grads


def on_device(
    atoms,
    distance_bins,
    bonds,
    molecule,
    block_counts,
    block_scaffold,
    pocket_ids,
    pocket_keys,
    pocket_values,
    pocket_bias,
    bin_table,
    bond_weight,
    w_query,
    w_key,
    w_value,
    w_out,
    w_cross_query,
    w_cross_out,
    cotangent,
):
    dp_count = lax.axis_size("dp")
    pocket_count = lax.axis_size("pocket")
    capacity = atoms.shape[0]
    balanced = cotangent.shape[0]
    row_count = atoms.shape[1]
    width = atoms.shape[2]
    heads = bin_table.shape[0]
    bin_count = bin_table.shape[1]
    per_target = -(-capacity // dp_count)
    pocket_rows = jnp.concatenate(
        [
            jnp.concatenate([pocket_keys, pocket_values], axis=1),
            jnp.pad(pocket_bias, ((0, extra_rows - heads), (0, 2 * width - pocket_bias.shape[1]))),
        ],
        axis=0,
    )
    pocket = lax.all_gather(pocket_rows, "pocket", axis=0)
    cross_bias = pocket[:, row_count : row_count + heads, None, :row_count].astype(jnp.float32)
    counts = lax.all_gather(block_counts.reshape(1), "dp", axis=0, tiled=True)
    places = lax.broadcasted_iota(jnp.int32, (dp_count, dp_count), 0)
    before = places > lax.broadcasted_iota(jnp.int32, (dp_count, dp_count), 1)
    offsets = jnp.sum(jnp.where(before, counts[None, :], 0), axis=1)
    own_device = lax.axis_index("dp")
    own_column = lax.axis_index("pocket")
    own_offset = offsets[own_device]
    own_count = counts[own_device]
    target_rows = lax.broadcasted_iota(jnp.int32, (dp_count, per_target), 0)
    turn_index = lax.broadcasted_iota(jnp.int32, (dp_count, per_target), 1)
    outgoing = jnp.mod(target_rows - own_offset, dp_count) + dp_count * turn_index
    picked = jnp.where(outgoing < own_count, outgoing, 0).reshape(-1)
    source_offset = offsets[:, None]
    source_count = counts[:, None]
    incoming = jnp.mod(own_device - source_offset, dp_count) + dp_count * turn_index
    usable = incoming < source_count
    landing = (source_offset + incoming) // dp_count
    wanted = lax.broadcasted_iota(jnp.int32, (balanced, 1), 0)
    matches = (landing.reshape(1, -1) == wanted) & usable.reshape(1, -1)
    received_index = lax.broadcasted_iota(jnp.int32, (balanced, dp_count * per_target), 1)
    position = jnp.sum(jnp.where(matches, received_index, 0), axis=1)
    anchors = ((target_rows * pocket_count + own_column) * capacity + incoming).reshape(1, -1)
    anchor = jnp.sum(jnp.where(matches, anchors, 0), axis=1)
    payload = pack_blocks(picked, atoms, distance_bins, bonds, molecule)
    got = lax.all_to_all(payload, "dp", split_axis=0, concat_axis=0, tiled=True)
    scaffold = pick(block_scaffold, anchor)
    ids = pocket_ids.T
    chosen = jnp.concatenate(
        [lax.dynamic_slice_in_dim(ids, scaffold[b], 1, 1)[:, 0] for b in range(balanced)]
    )
    table = jnp.concatenate(
        [
            bin_table,
            bin_table + bond_weight[:, None],
            jnp.full((heads, lanes - 2 * bin_count), masked_value, jnp.float32),
        ],
        axis=1,
    )
    table = lax.reduce_precision(table, 8, 7)[:, None, :]
    weights = (w_query, w_key, w_value, w_out, w_cross_query, w_cross_out)
    updated, early_grads, late_grads = layer(
        position, chosen, got, pocket, cross_bias, table, weights, cotangent.reshape(-1, width)
    )
    scale = 1.0 / math.sqrt(balanced * row_count * dp_count * pocket_count)

    def summed(grads):
        share = lax.psum_scatter(
            grads.reshape(-1, width), ("dp", "pocket"), scatter_dimension=0, tiled=True
        )
        share = (share.astype(jnp.float32) * scale).astype(jnp.bfloat16)
        return lax.all_gather(share, ("dp", "pocket"), axis=0, tiled=True).reshape(grads.shape)

    late = summed(late_grads)
    early = summed(early_grads)
    weight_grads = jnp.concatenate([early, late], axis=0)
    return (updated.reshape(cotangent.shape), weight_grads)


def solution(mesh):
    return jax.shard_map(
        on_device,
        mesh=mesh,
        in_specs=(
            P(("dp", "pocket"), None, None),
            P(("dp", "pocket"), None, None),
            P(("dp", "pocket"), None, None),
            P(("dp", "pocket"), None),
            P("dp", "pocket"),
            P(),
            P(),
            P("pocket", None),
            P("pocket", None),
            P(None, "pocket"),
            P(),
            P(),
            P(),
            P(),
            P(),
            P(),
            P(),
            P(),
            P(("dp", "pocket"), None, None),
        ),
        out_specs=(P(("dp", "pocket"), None, None), P()),
        check_vma=False,
    )
```
